32 devices in a mesh: gx: 4 (over z), gy: 2 (over y), gz: 4 (over x, core).
Axes of the slice: x: 2, y: 2, z: 4, core: 2. Of those that a mesh axis runs over, the one named last changes fastest.
Arguments:
- positions: float32 [4, 2, 4, 3, 128], P('gx', 'gy', 'gz'), may hold values from 0 to 5
- species: int32 [4, 2, 4, 128], P('gx', 'gy', 'gz'), may hold values from 0 to 5
- atom_count: int32 [4, 2, 4], P('gx', 'gy', 'gz'), may hold values from 16 to 128, as said below
- export_union: int32 [4, 2, 4, 64], P('gx', 'gy', 'gz'), may hold values from 0 to 127, as said below
- ghost_map: int32 [4, 2, 4, 27, 16], P('gx', 'gy', 'gz'), may hold values from 0 to 63, as said below
- edge_receiver: int32 [4, 2, 4, 1024], P('gx', 'gy', 'gz'), may hold values from 0 to 127, as said below
- edge_sender: int32 [4, 2, 4, 1024], P('gx', 'gy', 'gz'), may hold values from 0 to 559, as said below
- embed: float32 [6, 128], replicated, may hold values from -6 to 6
- species_energy: float32 [6], replicated, may hold values from -6 to 6
- radial_in: float32 [2, 8, 64], replicated, may hold values from -2 to 2
- radial_out: float32 [2, 64, 384], replicated, may hold values from -0.75 to 0.75
- mixing: float32 [2, 3, 128, 128], replicated, may hold values from -0.5 to 0.5
- product: float32 [2, 384, 128], replicated, may hold values from -0.3125 to 0.3125
- residual: float32 [2, 128, 128], replicated, may hold values from -0.5 to 0.5
- read_one: float32 [128], replicated, may hold values from -0.5 to 0.5
- read_hidden: float32 [128, 16], replicated, may hold values from -0.5 to 0.5
- read_two: float32 [16], replicated, may hold values from -1.5 to 1.5
Outputs:
- forces: float32 [4, 2, 4, 3, 128], P('gx', 'gy', 'gz')
- atom_energy: float32 [4, 2, 4, 128], P('gx', 'gy', 'gz')
- virial: float32 [3, 3], replicated
The draws below stay inside these ranges and needn't reach their ends.
Inputs may be any that keep to these rules, and one draw needn't show every extreme that they name: `atom_count`: the two middle layers of domains along gz are denser than the others, and one domain of them is full in every draw. `export_union`: every entry is a live atom of its own domain (below its count); entries may repeat. `ghost_map`: entry [k, s] is a position in the export_union of the neighbour at offset (k // 9 - 1, k // 3 % 3 - 1, k % 3 - 1) along (gx, gy, gz), all axes periodic. `edge_receiver`: edge slots below 8 times the domain's count are live and their receivers are live atoms; the other slots hold 0. `edge_sender`: A live sender below 128 is a live local atom; otherwise it is 128 + k * 16 + s, slot s of ghost block k, never k = 13. Padding slots hold 0.
All inputs are finite; a program needn't handle non-finite values.
Results may differ from the reference program's by a relative error of at most 0.0003.
Values sent between devices are 32-bit elements; how exact they have to be, the bound alone decides.
No kernel may reach another device: no remote copies, remote signals or barrier semaphores. Data moves between devices by JAX's collectives and lax.ppermute only.
A program may use at most 64 MiB of HBM per device.

```python
import jax
import jax.numpy as jnp
import numpy as np
from jax import lax

C = 128
NB = 8
RH = 64
RHID = 16
NSPEC = 6
DEG = 8
ATOMS_DEV = 128
EDGES = 1024
UNION = 64
GHOSTS = 16
DOMX = 4
DOMY = 2
DOMZ = 4


def domain_counts(key):
    base_key = jax.random.fold_in(key, 101)
    key_light, key_dense, key_full = jax.random.split(base_key, 3)
    light_counts = jax.random.randint(key_light, (DOMX, DOMY, DOMZ), ATOMS_DEV // 8, ATOMS_DEV // 3 + 1)
    dense_counts = jax.random.randint(key_dense, (DOMX, DOMY, DOMZ), ATOMS_DEV // 2, ATOMS_DEV + 1)
    layer_index = jnp.arange(DOMZ, dtype=jnp.int32)
    middle = (layer_index == DOMZ // 2 - 1) | (layer_index == DOMZ // 2)
    counts = jnp.where(middle[None, None, :], dense_counts, light_counts)
    chosen = jax.random.randint(key_full, (), 0, DOMX * DOMY)
    flat_spot = chosen * DOMZ + DOMZ // 2
    return counts.reshape(-1).at[flat_spot].set(ATOMS_DEV).reshape(DOMX, DOMY, DOMZ).astype(jnp.int32)


def draw_atom_count(key, part):
    return domain_counts(key)


def draw_export_union(key, part):
    counts = domain_counts(key)
    raw_bits = jax.random.randint(jax.random.fold_in(key, 102), (DOMX, DOMY, DOMZ, UNION), 0, 1 << 20)
    return (raw_bits % counts[..., None]).astype(jnp.int32)


def direction_lists(key):
    return jax.random.randint(jax.random.fold_in(key, 103), (DOMX, DOMY, DOMZ, 27, GHOSTS), 0, UNION).astype(jnp.int32)


def draw_ghost_map(key, part):
    direction_table = direction_lists(key)
    columns = []
    for direction in range(27):
        roll_shift = (1 - direction // 9, 1 - direction // 3 % 3, 1 - direction % 3)
        columns.append(jnp.roll(direction_table[:, :, :, 26 - direction, :], roll_shift, axis=(0, 1, 2)))
    return jnp.stack(columns, axis=3)


def edge_lists(key):
    counts = domain_counts(key)
    random_keys = jax.random.split(jax.random.fold_in(key, 104), 5)
    edge_shape = (DOMX, DOMY, DOMZ, EDGES)
    count_limit = counts[..., None]
    receiver = jax.random.randint(random_keys[0], edge_shape, 0, 1 << 20) % count_limit
    local_sender = jax.random.randint(random_keys[1], edge_shape, 0, 1 << 20) % count_limit
    ghost_block = jax.random.randint(random_keys[2], edge_shape, 0, 26)
    ghost_block = ghost_block + (ghost_block >= 13).astype(jnp.int32)
    ghost_slot = jax.random.randint(random_keys[3], edge_shape, 0, GHOSTS)
    remote = jax.random.randint(random_keys[4], edge_shape, 0, 2)
    sender = jnp.where(remote == 1, ATOMS_DEV + ghost_block * GHOSTS + ghost_slot, local_sender)
    edge_alive = jnp.arange(EDGES, dtype=jnp.int32)[None, None, None, :] < DEG * count_limit
    return (jnp.where(edge_alive, receiver, 0).astype(jnp.int32), jnp.where(edge_alive, sender, 0).astype(jnp.int32))


def draw_edge_receiver(key, part):
    return edge_lists(key)[0]


def draw_edge_sender(key, part):
    return edge_lists(key)[1]


def with_ends(entries, stream_key, low, high):
    longest = entries.shape.index(max(entries.shape))
    spots = []
    for shift in (0, 1):
        where = [jax.random.randint(jax.random.fold_in(stream_key, axis), (), 0, length) for axis, length in enumerate(entries.shape)]
        where[longest] = (where[longest] + shift) % entries.shape[longest]
        spots.append(tuple(where))
    return entries.at[spots[0]].set(low).at[spots[1]].set(high)


def block_levels(rng, extent, cuts, least, top_value):
    def one(position, shards_of):
        draws = jax.random.uniform(jax.random.fold_in(jax.random.fold_in(rng, 6), position), (shards_of,), jnp.float32, least / len(cuts), top_value / len(cuts))
        return jnp.repeat(jnp.exp(draws), extent[position] // shards_of).reshape((-1,) + (1,) * (len(extent) - position - 1))

    factor_of = one(*cuts[0])
    for cut in cuts[1:]:
        factor_of = factor_of * one(*cut)
    return factor_of


def bell_draw(own_key, dims, spread, bound, kind=jnp.bfloat16):
    values = spread * jax.random.normal(own_key, dims, jnp.float32)
    return jnp.clip(values, min=-bound, max=bound).astype(kind)


def setup_inputs(seed: int = 0) -> dict:
    arg_keys = jax.random.split(jax.random.key(seed), 18)
    positions = jnp.clip(5.0 * jax.random.uniform(arg_keys[0], (DOMX, DOMY, DOMZ, 3, ATOMS_DEV), jnp.float32) ** block_levels(arg_keys[0], (DOMX, DOMY, DOMZ, 3, ATOMS_DEV), ((0, 4), (1, 2), (2, 4)), -0.2, 0.2), 0.0, 5.0)
    species = with_ends(jax.random.randint(arg_keys[1], (DOMX, DOMY, DOMZ, ATOMS_DEV), 0, NSPEC), jax.random.fold_in(arg_keys[1], 1), 0, NSPEC - 1).astype(jnp.int32)
    atom_count = draw_atom_count(jax.random.fold_in(arg_keys[17], 71), 0)
    export_union = draw_export_union(jax.random.fold_in(arg_keys[17], 71), 0)
    ghost_map = draw_ghost_map(jax.random.fold_in(arg_keys[17], 71), 0)
    edge_receiver = draw_edge_receiver(jax.random.fold_in(arg_keys[17], 71), 0)
    edge_sender = draw_edge_sender(jax.random.fold_in(arg_keys[17], 71), 0)
    embed = bell_draw(arg_keys[7], (NSPEC, C), 1.0, 6.0, jnp.float32)
    species_energy = bell_draw(arg_keys[8], (NSPEC,), 1.0, 6.0, jnp.float32)
    radial_in = bell_draw(arg_keys[9], (2, NB, RH), NB ** -0.5, 2.0, jnp.float32)
    radial_out = bell_draw(arg_keys[10], (2, RH, 3 * C), RH ** -0.5, 0.75, jnp.float32)
    mixing = bell_draw(arg_keys[11], (2, 3, C, C), C ** -0.5, 0.5, jnp.float32)
    product = bell_draw(arg_keys[12], (2, 3 * C, C), (3 * C) ** -0.5, 0.3125, jnp.float32)
    residual = bell_draw(arg_keys[13], (2, C, C), C ** -0.5, 0.5, jnp.float32)
    read_one = bell_draw(arg_keys[14], (C,), C ** -0.5, 0.5, jnp.float32)
    read_hidden = bell_draw(arg_keys[15], (C, RHID), C ** -0.5, 0.5, jnp.float32)
    read_two = bell_draw(arg_keys[16], (RHID,), RHID ** -0.5, 1.5, jnp.float32)
    return {"positions": positions, "species": species, "atom_count": atom_count, "export_union": export_union, "ghost_map": ghost_map, "edge_receiver": edge_receiver, "edge_sender": edge_sender, "embed": embed, "species_energy": species_energy, "radial_in": radial_in, "radial_out": radial_out, "mixing": mixing, "product": product, "residual": residual, "read_one": read_one, "read_hidden": read_hidden, "read_two": read_two}


DOMAIN_SIDE = 5.0
SOFTENING = 0.25
RADIAL_RANGE = 18.0
ROOT_THREE = 3.0 ** 0.5
ROOT_FIVE = 5.0 ** 0.5
ROOT_FIFTEEN = 15.0 ** 0.5
COMPONENT_DEGREE = np.array([0, 1, 1, 1, 2, 2, 2, 2, 2], dtype=np.int32)
FULL_PRECISION = lax.Precision.HIGHEST

def harmonics(unit):
    along_x, along_y, along_z = (unit[0], unit[1], unit[2])
    return jnp.stack([jnp.ones_like(along_x), ROOT_THREE * along_x, ROOT_THREE * along_y, ROOT_THREE * along_z, ROOT_FIFTEEN * along_x * along_y, ROOT_FIFTEEN * along_y * along_z, 0.5 * ROOT_FIVE * (3.0 * along_z * along_z - 1.0), ROOT_FIFTEEN * along_x * along_z, 0.5 * ROOT_FIFTEEN * (along_x * along_x - along_y * along_y)])

def offset_table(ghost_count):
    direction = np.arange(27)
    offsets = np.stack([direction // 9 - 1, direction // 3 % 3 - 1, direction % 3 - 1]).astype(np.float32) * DOMAIN_SIDE
    return jnp.asarray(np.repeat(offsets, ghost_count, axis=1))

def neighbour_table():
    domain = np.arange(DOMX * DOMY * DOMZ)
    along_x = domain // (DOMY * DOMZ)
    along_y = domain // DOMZ % DOMY
    along_z = domain % DOMZ
    columns = []
    for direction in range(27):
        step_x = direction // 9 - 1
        step_y = direction // 3 % 3 - 1
        step_z = direction % 3 - 1
        columns.append(((along_x + step_x) % DOMX * DOMY + (along_y + step_y) % DOMY) * DOMZ + (along_z + step_z) % DOMZ)
    return np.stack(columns, axis=1).astype(np.int32)

def edge_terms(h_table, coord_table, strain, receiver, sender, edge_live, radial_in, radial_out, atom_slots):
    separation = coord_table[:, sender] - coord_table[:, receiver]
    separation = separation + jnp.dot(strain, separation, precision=FULL_PRECISION)
    length = jnp.sqrt(lax.optimization_barrier(jnp.sum(separation * separation, axis=0)) + SOFTENING)
    unit = separation / length[None, :]
    angular = harmonics(unit)
    orders = jnp.arange(1, radial_in.shape[0] + 1, dtype=jnp.int32).astype(jnp.float32)[:, None]
    radial_basis = (2.0 / RADIAL_RANGE) ** 0.5 * jnp.sin(orders * (jnp.pi / RADIAL_RANGE) * length[None, :]) / length[None, :]
    hidden = jax.nn.silu(jnp.dot(radial_in.T, radial_basis, precision=FULL_PRECISION))
    channels = h_table.shape[0]
    radial = jnp.dot(radial_out.T, hidden, precision=FULL_PRECISION).reshape(3, channels, -1)
    per_component = radial[COMPONENT_DEGREE]
    message = per_component * angular[:, None, :] * (h_table[:, sender] * edge_live[None, :])[None]
    return jnp.zeros((9, channels, atom_slots), jnp.float32).at[:, :, receiver].add(message)

def interact(h_table, coord_table, strain, receiver, sender, edge_live, radial_in, radial_out, mixing, product, residual, atom_slots):
    edge_count = receiver.shape[0]
    block_size = min(1024, edge_count)
    block_count = edge_count // block_size
    channels = h_table.shape[0]

    def block_sum(receiver_part, sender_part, live_part):
        return edge_terms(h_table, coord_table, strain, receiver_part, sender_part, live_part, radial_in, radial_out, atom_slots)
    checked = jax.checkpoint(block_sum)

    def advance(summed, inputs):
        return (summed + checked(inputs[0], inputs[1], inputs[2]), None)
    start = jnp.zeros((9, channels, atom_slots), jnp.float32)
    summed, unused = lax.scan(advance, start, (receiver.reshape(block_count, block_size), sender.reshape(block_count, block_size), edge_live.reshape(block_count, block_size)))
    summed = summed * float(DEG) ** (-0.5)
    scalar_part = jnp.dot(mixing[0].T, summed[0], precision=FULL_PRECISION)
    vector_mix = jnp.einsum('dc,mda->mca', mixing[1], summed[1:4], precision=FULL_PRECISION)
    tensor_mix = jnp.einsum('dc,mda->mca', mixing[2], summed[4:9], precision=FULL_PRECISION)
    invariants = jnp.concatenate([scalar_part, lax.optimization_barrier(jnp.sum(vector_mix * vector_mix, axis=0)), lax.optimization_barrier(jnp.sum(tensor_mix * tensor_mix, axis=0))], axis=0)
    return jnp.dot(product.T, invariants, precision=FULL_PRECISION) + jnp.dot(residual.T, h_table[:, :atom_slots], precision=FULL_PRECISION)

def reference(positions, species, atom_count, export_union, ghost_map, edge_receiver, edge_sender, embed, species_energy, radial_in, radial_out, mixing, product, residual, read_one, read_hidden, read_two):
    domains = DOMX * DOMY * DOMZ
    coords = positions.reshape(domains, 3, ATOMS_DEV)
    species_flat = species.reshape(domains, ATOMS_DEV)
    counts = atom_count.reshape(domains)
    union_rows = export_union.reshape(domains, UNION)
    ghost_rows = ghost_map.reshape(domains, 27, GHOSTS)
    receivers = edge_receiver.reshape(domains, EDGES)
    senders = edge_sender.reshape(domains, EDGES)
    neighbour_of = jnp.asarray(neighbour_table()).astype(jnp.int32)
    ghost_domain = jnp.broadcast_to(neighbour_of[:, :, None], (domains, 27, GHOSTS)).reshape(domains, 27 * GHOSTS)
    ghost_atom = union_rows[neighbour_of[:, :, None], ghost_rows].reshape(domains, 27 * GHOSTS)
    onehot = (species_flat[:, None, :] == jnp.arange(NSPEC, dtype=jnp.int32)[None, :, None]).astype(jnp.float32)
    atom_live = (jnp.arange(ATOMS_DEV, dtype=jnp.int32)[None, :] < counts[:, None]).astype(jnp.float32)
    edge_live = (jnp.arange(EDGES, dtype=jnp.int32)[None, :] < DEG * counts[:, None]).astype(jnp.float32)
    onehot_table = jnp.concatenate([onehot, jnp.swapaxes(onehot[ghost_domain, :, ghost_atom], 1, 2)], axis=2)
    h0_tables = jnp.einsum('sc,dsa->dca', embed, onehot_table, precision=FULL_PRECISION)
    shifts = offset_table(GHOSTS)

    def apply_layer(h_tables, coord_tables, strain, layer_index):

        def one_domain(inputs):
            return interact(inputs[0], inputs[1], strain, inputs[2], inputs[3], inputs[4], radial_in[layer_index], radial_out[layer_index], mixing[layer_index], product[layer_index], residual[layer_index], ATOMS_DEV)
        return lax.map(jax.checkpoint(one_domain), (h_tables, coord_tables, receivers, senders, edge_live))

    def energy(coords, strain):
        ghost_coords = jnp.swapaxes(coords[ghost_domain, :, ghost_atom], 1, 2) + shifts[None]
        coord_tables = jnp.concatenate([coords, ghost_coords], axis=2)
        first = apply_layer(h0_tables, coord_tables, strain, 0)
        ghost_first = jnp.swapaxes(first[ghost_domain, :, ghost_atom], 1, 2)
        second = apply_layer(jnp.concatenate([first, ghost_first], axis=2), coord_tables, strain, 1)
        energy_one = jnp.einsum('c,dca->da', read_one, first, precision=FULL_PRECISION)
        hidden_read = jax.nn.silu(jnp.einsum('ck,dca->dka', read_hidden, second, precision=FULL_PRECISION))
        energy_two = jnp.einsum('k,dka->da', read_two, hidden_read, precision=FULL_PRECISION)
        base_energy = jnp.einsum('s,dsa->da', species_energy, onehot, precision=FULL_PRECISION)
        per_atom = (base_energy + energy_one + energy_two) * atom_live
        return (jnp.sum(per_atom), per_atom)
    (total, per_atom), (coord_grad, strain_grad) = jax.value_and_grad(energy, argnums=(0, 1), has_aux=True)(coords, jnp.zeros((3, 3), jnp.float32))
    forces = -coord_grad.reshape(positions.shape)
    virial = -strain_grad / jnp.sum(counts).astype(jnp.float32)
    return (forces, per_atom.reshape(species.shape), virial)
```

```python
import functools

import jax
import jax.numpy as jnp
import numpy as np
from jax import lax
from jax.experimental import pallas as pl
from jax.experimental.pallas import tpu as pltpu
from jax.sharding import PartitionSpec as P

DEG = 8
DOMAIN_SIDE = 5.0
SOFTENING = 0.25
RADIAL_RANGE = 18.0
R3 = 3.0**0.5
R5 = 5.0**0.5
R15 = 15.0**0.5
F32 = jnp.float32
BF16 = jnp.bfloat16
DEGREE = (0, 1, 1, 1, 2, 2, 2, 2, 2)
TILE = 256
AXES = ("gx", "gy", "gz")


def split(x, parts):
    out = []
    for i in range(parts):
        piece = x.astype(BF16)
        out.append(piece)
        if i + 1 < parts:
            x = x - piece.astype(F32)
    return out


def mm(a, b):
    return lax.dot_general(a, b, (((1,), (0,)), ((), ())), preferred_element_type=F32)


def mm_nt(a, b):
    return lax.dot_general(a, b, (((1,), (1,)), ((), ())), preferred_element_type=F32)


def stack3(x):
    hi, lo = split(x, 2)
    return jnp.concatenate([hi, hi, lo], axis=0)


def iota(shape, dim):
    return lax.broadcasted_iota(jnp.int32, shape, dim)


def onehot(row, size):
    return jnp.where(iota((size, row.shape[1]), 0) == row, 1.0, 0.0).astype(BF16)


def wide(x):
    hi = lax.reduce_precision(x, 8, 7)
    return jnp.concatenate([hi, x - hi, hi], axis=-1).astype(BF16)


def wide_exact(x):
    hi = lax.reduce_precision(x, 8, 7)
    mid = lax.reduce_precision(x - hi, 8, 7)
    return jnp.concatenate([hi, mid, x - hi - mid], axis=-1).astype(BF16)


def sin_cos(theta):
    shift = theta - np.float32(np.pi / 2)
    square = shift * shift
    even, odd = [1.0], [1.0]
    for n in range(1, 9):
        even.append(-even[-1] / ((2 * n - 1) * (2 * n)))
        odd.append(-odd[-1] / ((2 * n) * (2 * n + 1)))
    cos_shift = jnp.full_like(theta, even[-1])
    sin_shift = jnp.full_like(theta, odd[-1])
    for n in range(7, -1, -1):
        cos_shift = cos_shift * square + np.float32(even[n])
        sin_shift = sin_shift * square + np.float32(odd[n])
    return cos_shift, -(sin_shift * shift)


def geometry(sep):
    length = jnp.sqrt(sep[0] * sep[0] + sep[1] * sep[1] + sep[2] * sep[2] + SOFTENING)
    inverse = 1.0 / length
    return length, inverse, [s * inverse for s in sep]


def harmonics(unit):
    a, b, c = unit
    return [
        None,
        R3 * a,
        R3 * b,
        R3 * c,
        R15 * a * b,
        R15 * b * c,
        (0.5 * R5) * (3.0 * c * c - 1.0),
        R15 * a * c,
        (0.5 * R15) * (a * a - b * b),
    ]


def bases(length, inverse, count):
    step = np.float32(np.pi / RADIAL_RANGE)
    sine, cosine = sin_cos(length * step)
    twice = 2.0 * cosine
    s_before, s_now = jnp.zeros_like(sine), sine
    c_before, c_now = jnp.ones_like(sine), cosine
    front = np.float32((2.0 / RADIAL_RANGE) ** 0.5) * inverse
    values, slopes = [], []
    for n in range(1, count + 1):
        value = front * s_now
        values.append(value)
        slopes.append(front * (n * step) * c_now - value * inverse)
        s_before, s_now = s_now, twice * s_now - s_before
        c_before, c_now = c_now, twice * c_now - c_before
    return jnp.concatenate(values, axis=0), jnp.concatenate(slopes, axis=0)


def stack3_rows(x):
    hi = x.astype(BF16).astype(F32)
    return jnp.concatenate([hi, hi, x - hi], axis=0).astype(BF16)


def radial_net(rin, rout, value, slope):
    both = jnp.concatenate([stack3_rows(value), stack3_rows(slope)], axis=1)
    width = value.shape[1]
    first = mm(rin, both)
    pre, pre_slope = first[:, :width], first[:, width:]
    gate = 1.0 / (1.0 + jnp.exp(-pre))
    hidden = pre * gate
    hidden_slope = gate * (1.0 + pre * (1.0 - gate)) * pre_slope
    second = mm(rout, jnp.concatenate([stack3(hidden), stack3(hidden_slope)], axis=1))
    return second[:, :width], second[:, width:]


def rows_of(ref, where, count):
    block = ref[:, where]
    return [block[i : i + 1] for i in range(count)]


def forward_tile(where, sep_ref, basis_ref, slope_ref, live_row, rin, rout, features, w_ref, wp_ref, rad_ref, agg_ref):
    channels = features.shape[0]
    atoms = agg_ref.shape[1]
    length, inverse, unit = geometry(rows_of(sep_ref, where, 3))
    angular = harmonics(unit)
    rad, rad_slope = radial_net(rin, rout, basis_ref[:, where], slope_ref[:, where])
    weighted = []
    for l in range(3):
        part = slice(l * channels, (l + 1) * channels)
        weighted.append(rad[part] * features)
        w_ref[part, where] = weighted[l]
        wp_ref[part, where] = rad_slope[part] * features
    if rad_ref is not None:
        rad_ref[:, where] = rad
    pick = onehot(live_row, atoms)
    pick = jnp.concatenate([pick, pick], axis=1)
    for m, l in enumerate(DEGREE):
        message = weighted[l] if m == 0 else weighted[l] * angular[m]
        part = slice(m * channels, (m + 1) * channels)
        agg_ref[part, :] += mm_nt(jnp.concatenate(split(message, 2), axis=1), pick)


def mix_forward(agg_ref, mixed_ref, mix_ref, tail_ref, h_local):
    channels, atoms = h_local.shape
    scale = float(DEG) ** -0.5
    squares = []
    for l, ms in enumerate(((0,), (1, 2, 3), (4, 5, 6, 7, 8))):
        stacked = jnp.concatenate([agg_ref[m * channels : (m + 1) * channels, :] * scale for m in ms], axis=1)
        mixed = mm(mix_ref[l], stack3(stacked))
        total = None
        for i, m in enumerate(ms):
            piece = mixed[:, i * atoms : (i + 1) * atoms]
            mixed_ref[m * channels : (m + 1) * channels, :] = piece
            term = piece if l == 0 else piece * piece
            total = term if total is None else total + term
        squares.append(total)
    return mm(tail_ref[...], stack3(jnp.concatenate(squares + [h_local], axis=0)))


def mix_backward(grad, mixed_ref, back_mix_ref, back_tail_ref, dagg_ref):
    channels, atoms = grad.shape
    scale = float(DEG) ** -0.5
    spread = mm(back_tail_ref[...], stack3(grad))
    for l, ms in enumerate(((0,), (1, 2, 3), (4, 5, 6, 7, 8))):
        base = spread[l * channels : (l + 1) * channels]
        pieces = []
        for m in ms:
            if l == 0:
                pieces.append(base * scale)
            else:
                pieces.append(base * (mixed_ref[m * channels : (m + 1) * channels, :] * (2.0 * scale)))
        out = mm(back_mix_ref[l], stack3(jnp.concatenate(pieces, axis=1)))
        for i, m in enumerate(ms):
            piece = out[:, i * atoms : (i + 1) * atoms]
            dagg_ref[m * channels : (m + 1) * channels, :] = jnp.concatenate(split(piece, 2), axis=1)
    return spread[3 * channels :]


def backward_tile(where, sep_ref, live_row, dagg_ref, w_ref, wp_ref, rad_ref, out_ref):
    channels = w_ref.shape[0] // 3
    atoms = dagg_ref.shape[1] // 2
    length, inverse, unit = geometry(rows_of(sep_ref, where, 3))
    angular = harmonics(unit)
    pick = onehot(live_row, atoms)
    pick = jnp.concatenate([pick, pick], axis=0)
    by_weight = [None, None, None]
    by_angle = [None] * 9
    for m, l in enumerate(DEGREE):
        grad = mm(dagg_ref[m * channels : (m + 1) * channels, :], pick)
        term = grad if m == 0 else grad * angular[m]
        by_weight[l] = term if by_weight[l] is None else by_weight[l] + term
        if m:
            by_angle[m] = jnp.sum(grad * w_ref[l * channels : (l + 1) * channels, where], axis=0, keepdims=True)
    total, feature_grad = None, None
    for l in range(3):
        part = slice(l * channels, (l + 1) * channels)
        term = by_weight[l] * wp_ref[part, where]
        total = term if total is None else total + term
        if rad_ref is not None:
            term = by_weight[l] * rad_ref[part, where]
            feature_grad = term if feature_grad is None else feature_grad + term
    by_length = jnp.sum(total, axis=0, keepdims=True)
    a, b, c = unit
    p = by_angle
    by_unit = [
        R3 * p[1] + R15 * (b * p[4] + c * p[7] + a * p[8]),
        R3 * p[2] + R15 * (a * p[4] + c * p[5] - b * p[8]),
        R3 * p[3] + R15 * (b * p[5] + a * p[7]) + (3.0 * R5) * c * p[6],
    ]
    along = a * by_unit[0] + b * by_unit[1] + c * by_unit[2]
    for i in range(3):
        out_ref[i : i + 1, where] = (by_unit[i] - unit[i] * along) * inverse + by_length * unit[i]
    return feature_grad


def live_receiver(recv, count):
    return jnp.where(iota(recv.shape, 1) < DEG * count, recv, -1)


def tiles(total, body):
    def step(i, carry):
        body(pl.ds(pl.multiple_of(i * TILE, TILE), TILE))
        return carry

    lax.fori_loop(0, total // TILE, step, 0)


def first_kernel(plan, refs):
    n_in = len(plan.groups) + 3
    packs, refs = refs[:n_in], refs[n_in:]
    (count_ref, recv_ref, send_ref, emb_ref, se_ref, rin_ref, rout_ref, mix_ref, tail_ref, one_ref) = refs[:10]
    (minus_ref, zero_ref, plus_ref, h_ref, mixed_ref, sep_ref, energy_ref, list_ref) = refs[10:18]
    all_ref, basis_ref, slope_ref, live_ref, w_ref, wp_ref, agg_ref, species_ref = refs[18:]
    ghosts, union = plan.ghosts, plan.union
    blocks = 27
    lanes = blocks * ghosts
    atoms = agg_ref.shape[1]
    count = count_ref[0]
    own = packs[1][...]
    for k in range(blocks):
        i, q = k // 9, k % 9
        if q == 4:
            piece = packs[i][...]
        else:
            piece = packs[3 + plan.source[q]][8 * i : 8 * i + 8, :]
        all_ref[8 * k : 8 * k + 8, :] = piece
    flat = (iota((8, 128), 0) - 4) * 128 + iota((8, 128), 1)
    asked = jnp.zeros((8, 128), F32)
    for k in range(blocks):
        lo = (26 - k) * ghosts
        asked = jnp.where((flat >= lo) & (flat < lo + ghosts), all_ref[8 * k : 8 * k + 8, :], asked)

    def flat_lists(pack):
        rows = jnp.concatenate([pack[r : r + 1] for r in range(4, 8)], axis=1)
        return rows[:, :lanes].astype(jnp.int32)

    offers = mm(all_ref[...].astype(BF16), onehot(flat_lists(own) + (128 - union), 128))
    block_of = iota((8, lanes), 1) // ghosts
    chosen = jnp.zeros((8, lanes), F32)
    for k in range(blocks):
        chosen = jnp.where(block_of == k, offers[8 * k : 8 * k + 8], chosen)
    ghost_atom = chosen[7:8].astype(jnp.int32)
    mine = mm(own.astype(BF16), onehot(flat_lists(asked) + (128 - union), 128))
    send_atom = mine[7:8].astype(jnp.int32)
    list_ref[...] = jnp.broadcast_to(send_atom, (8, lanes))
    found = None
    pick = onehot(ghost_atom, 128)
    for piece in split(all_ref[...], 3):
        term = mm(piece, pick)
        found = term if found is None else found + term
    table = jnp.zeros((8, lanes), F32)
    row = iota((8, lanes), 0)
    for k in range(blocks):
        table = jnp.where(block_of == k, found[8 * k : 8 * k + 8], table)
    offset = jnp.where(row == 0, block_of // 9 - 1, jnp.where(row == 1, block_of // 3 % 3 - 1, block_of % 3 - 1))
    table = jnp.where(row < 3, table + DOMAIN_SIDE * offset.astype(F32), table)
    table = jnp.concatenate([own, table], axis=1)
    table = jnp.concatenate(split(table, 3), axis=0)
    own3 = jnp.concatenate(split(own, 3), axis=0)
    edges = recv_ref.shape[1]
    from_sender = mm(table, onehot(send_ref[...], table.shape[1]))
    at_receiver = mm(own3, onehot(recv_ref[...], atoms))
    from_sender = (from_sender[16:] + from_sender[8:16]) + from_sender[:8]
    at_receiver = (at_receiver[16:] + at_receiver[8:16]) + at_receiver[:8]
    sep_ref[...] = from_sender - jnp.where(iota((8, edges), 0) < 3, at_receiver, 0.0)
    species_ref[...] = from_sender[3:4].astype(jnp.int32)
    length, inverse, unit = geometry([sep_ref[i : i + 1, :] for i in range(3)])
    value, slope = bases(length, inverse, rin_ref.shape[1] // 3)
    basis_ref[...] = value
    slope_ref[...] = slope
    live_ref[...] = live_receiver(recv_ref[...], count)
    agg_ref[...] = jnp.zeros_like(agg_ref)

    def species_features(row):
        hot = jnp.where(iota((8, row.shape[1]), 0) == row, 1.0, 0.0)
        return mm(emb_ref[...], jnp.concatenate([hot, hot, hot], axis=0).astype(BF16)), hot

    def body(where):
        features, unused = species_features(species_ref[:, where])
        forward_tile(
            where, sep_ref, basis_ref, slope_ref, live_ref[:, where], rin_ref[...], rout_ref[...], features,
            w_ref, wp_ref, None, agg_ref,
        )

    tiles(edges, body)
    h0, hot = species_features(own[3:4].astype(jnp.int32))
    h1 = mix_forward(agg_ref, mixed_ref, mix_ref, tail_ref, h0)
    h_ref[...] = h1
    parts = split(h1, 2)
    chosen_h = mm_nt(onehot_rows(send_atom, atoms), jnp.concatenate(parts, axis=0))
    chosen_h = chosen_h[:, :128] + chosen_h[:, 128:]
    third = 9 * ghosts
    minus_ref[...] = chosen_h[:third]
    zero_ref[...] = chosen_h[third : 2 * third]
    plus_ref[...] = chosen_h[2 * third :]
    energy = jnp.sum(hot * se_ref[...], axis=0, keepdims=True) + jnp.sum(h1 * one_ref[...], axis=0, keepdims=True)
    energy_ref[...] = jnp.broadcast_to(energy, (8, atoms))


def onehot_rows(row, size):
    hot = jnp.where(iota((size, row.shape[1]), 0) == row, 1.0, 0.0)
    pad = (-row.shape[1]) % 128
    if pad:
        hot = jnp.concatenate([hot, jnp.zeros((size, pad), F32)], axis=1)
    return hot.T[: row.shape[1]].astype(BF16)


def second_kernel(plan, refs):
    n_in = len(plan.groups) + 2
    got, refs = refs[:n_in], refs[n_in:]
    (count_ref, recv_ref, send_ref, h_ref, sep_ref, energy_ref, rin_ref, rout_ref, mix_ref, tail_ref) = refs[:10]
    (back_mix_ref, back_tail_ref, read_ref, back_read_ref, two_ref, one_ref) = refs[10:16]
    (minus_ref, zero_ref, plus_ref, dlocal_ref, base_ref, edge_ref, out_energy_ref) = refs[16:23]
    (table_ref, basis_ref, slope_ref, live_ref, w_ref, wp_ref, rad_ref, agg_ref, mixed_ref, dagg_ref, dt_ref) = refs[23:]
    ghosts = plan.ghosts
    atoms = agg_ref.shape[1]
    channels = h_ref.shape[0]
    count = count_ref[0]
    edges = recv_ref.shape[1]
    h1 = h_ref[...]
    table_ref[:, :atoms] = jnp.concatenate(split(h1, 2), axis=0)
    rows = ghost_rows(plan, got, ghosts, channels)
    lanes = 27 * ghosts
    pad = (-lanes) % 128
    ghost = jnp.concatenate(rows + [jnp.zeros((pad, channels), F32)], axis=0).T
    table_ref[:, atoms:] = jnp.concatenate(split(ghost, 2), axis=0)[:, :lanes]
    length, inverse, unit = geometry([sep_ref[i : i + 1, :] for i in range(3)])
    value, slope = bases(length, inverse, rin_ref.shape[1] // 3)
    basis_ref[...] = value
    slope_ref[...] = slope
    live_ref[...] = live_receiver(recv_ref[...], count)
    agg_ref[...] = jnp.zeros_like(agg_ref)
    slots = atoms + lanes

    def body(where):
        features = mm(table_ref[...], onehot(send_ref[:, where], slots))
        features = features[:channels] + features[channels:]
        forward_tile(
            where, sep_ref, basis_ref, slope_ref, live_ref[:, where], rin_ref[...], rout_ref[...], features,
            w_ref, wp_ref, rad_ref, agg_ref,
        )

    tiles(edges, body)
    h2 = mix_forward(agg_ref, mixed_ref, mix_ref, tail_ref, h1)
    pre = mm(read_ref[...], stack3(h2))
    gate = 1.0 / (1.0 + jnp.exp(-pre))
    live = jnp.where(iota((1, atoms), 1) < count, 1.0, 0.0)
    energy_two = jnp.sum(two_ref[...] * (pre * gate), axis=0, keepdims=True)
    out_energy_ref[...] = (energy_ref[...] + energy_two) * live
    grad_pre = two_ref[...] * (gate * (1.0 + pre * (1.0 - gate))) * live
    grad = mm(back_read_ref[...], stack3(grad_pre))
    base_ref[...] = mix_backward(grad, mixed_ref, back_mix_ref, back_tail_ref, dagg_ref) + one_ref[...] * live
    dt_ref[...] = jnp.zeros_like(dt_ref)
    edge_ref[...] = jnp.zeros_like(edge_ref)

    def back(where):
        feature_grad = backward_tile(
            where, sep_ref, live_ref[:, where], dagg_ref, w_ref, wp_ref, rad_ref, edge_ref
        )
        dt_ref[...] += mm_nt(onehot(send_ref[:, where], slots), jnp.concatenate(split(feature_grad, 2), axis=0))

    tiles(edges, back)
    grads = dt_ref[:, :channels] + dt_ref[:, channels:]
    third = 9 * ghosts
    dlocal_ref[...] = grads[:atoms]
    minus_ref[...] = grads[atoms : atoms + third]
    zero_ref[...] = grads[atoms + third : atoms + 2 * third]
    plus_ref[...] = grads[atoms + 2 * third :]


def ghost_rows(plan, got, size, width):
    rows = []
    for k in range(27):
        i, q = k // 9, k % 9
        if k == 13:
            rows.append(jnp.zeros((size, width), F32))
        elif q == 4:
            rows.append(got[0 if i == 0 else 1][4 * size : 5 * size, :])
        else:
            group, place = plan.place[q]
            at = (3 * place + i) * size
            rows.append(got[2 + group][at : at + size, :])
    return rows


def third_kernel(plan, refs):
    n_in = len(plan.groups) + 2
    got, refs = refs[:n_in], refs[n_in:]
    (count_ref, recv_ref, send_ref, own_ref, dlocal_ref, base_ref, edge_in_ref, sep_ref, mixed_ref, list_ref) = refs[:10]
    (emb_ref, rin_ref, rout_ref, back_mix_ref, back_tail_ref) = refs[10:15]
    minus_ref, zero_ref, plus_ref, grads_ref, strain_ref = refs[15:20]
    (live_ref, basis_ref, slope_ref, w_ref, wp_ref, dagg_ref, edge_ref) = refs[20:]
    ghosts = plan.ghosts
    atoms = own_ref.shape[1]
    channels = base_ref.shape[0]
    edges = recv_ref.shape[1]
    lanes = 27 * ghosts
    count = count_ref[0]
    returned = jnp.concatenate(ghost_rows(plan, got, ghosts, channels), axis=0)
    pick = onehot(list_ref[0:1, :], atoms)
    back = mm(pick, jnp.concatenate(split(returned, 2), axis=1))
    back = dlocal_ref[...] + back[:, :channels] + back[:, channels:]
    grad = base_ref[...] + back.T
    mix_backward(grad, mixed_ref, back_mix_ref, back_tail_ref, dagg_ref)
    length, inverse, unit = geometry([sep_ref[i : i + 1, :] for i in range(3)])
    value, slope = bases(length, inverse, rin_ref.shape[1] // 3)
    live_ref[...] = live_receiver(recv_ref[...], count)
    basis_ref[...] = value
    slope_ref[...] = slope

    def body(where):
        species = sep_ref[:, where][3:4].astype(jnp.int32)
        hot = jnp.where(iota((8, TILE), 0) == species, 1.0, 0.0)
        features = mm(emb_ref[...], jnp.concatenate([hot, hot, hot], axis=0).astype(BF16))
        rad, rad_slope = radial_net(rin_ref[...], rout_ref[...], basis_ref[:, where], slope_ref[:, where])
        for l in range(3):
            part = slice(l * channels, (l + 1) * channels)
            w_ref[part, where] = rad[part] * features
            wp_ref[part, where] = rad_slope[part] * features
        backward_tile(where, sep_ref, live_ref[:, where], dagg_ref, w_ref, wp_ref, None, edge_ref)

    tiles(edges, body)
    edge = [edge_ref[i : i + 1, :] + edge_in_ref[i : i + 1, :] for i in range(3)]
    sep = [sep_ref[i : i + 1, :] for i in range(3)]
    sender = send_ref[...]
    by_atom = jnp.where(iota((atoms, edges), 0) == sender, 1.0, 0.0) - jnp.where(
        iota((atoms, edges), 0) == recv_ref[...], 1.0, 0.0
    )
    five = [jnp.zeros_like(edge[0])] * 5
    stacked = jnp.concatenate(split(jnp.concatenate(edge + five, axis=0), 3), axis=0)
    sums = mm_nt(stacked, by_atom.astype(BF16))
    grads_ref[...] = (sums[16:] + sums[8:16]) + sums[:8]
    ghost = sender - atoms
    block = jnp.where(ghost >= 0, ghost // ghosts, -1)
    slot = ghost % ghosts
    slot_hot = jnp.where(iota((ghosts, edges), 0) == slot, 1.0, 0.0)
    spread = jnp.concatenate([g * slot_hot for g in edge], axis=0)
    pad = jnp.zeros((128 - 3 * ghosts, edges), F32)
    pieces = split(jnp.concatenate([spread, pad], axis=0), 3)
    for i, out in enumerate((minus_ref, zero_ref, plus_ref)):
        rows = iota((16, edges), 0)
        hot = jnp.where((rows + 9 * i == block) & (rows < 9), 1.0, 0.0).astype(BF16)
        sums = [mm_nt(hot, piece) for piece in pieces]
        out[...] = (sums[2] + sums[1]) + sums[0]
    row, lane = iota((8, 128), 0), iota((8, 128), 1)
    packed = jnp.where((row == 3) & (lane == 0), count.astype(F32), 0.0)
    for i in range(3):
        for j in range(3):
            packed = jnp.where((row == i) & (lane == j), jnp.sum(edge[i] * sep[j]), packed)
    strain_ref[...] = packed


def last_kernel(plan, refs):
    n_in = len(plan.groups) + 2
    got, refs = refs[:n_in], refs[n_in:]
    n_strain = plan.n_strain
    strains, refs = refs[:n_strain], refs[n_strain:]
    grads_ref, list_ref, force_ref, virial_ref = refs
    ghosts = plan.ghosts
    lanes = 27 * ghosts
    atoms = grads_ref.shape[1]
    rows = []
    for k in range(27):
        i, q = k // 9, k % 9
        if k == 13:
            rows.append(jnp.zeros((1, 128), F32))
        elif q == 4:
            rows.append(got[0 if i == 0 else 1][4:5, :])
        else:
            at = 16 * i + q
            rows.append(got[2 + plan.place[q][0]][at : at + 1, :])
    block = jnp.concatenate(rows + [jnp.zeros((5, 128), F32)], axis=0)
    block = jnp.concatenate(split(block, 3), axis=1)
    repeat = jnp.where(iota((lanes, 32), 0) // ghosts == iota((lanes, 32), 1), 1.0, 0.0).astype(BF16)
    tall = mm(repeat, block)
    keep = iota((lanes, 384), 0) % ghosts == iota((lanes, 384), 1) % ghosts
    tall = jnp.where(keep, tall, 0.0).astype(BF16)
    summed = mm(onehot(list_ref[0:1, :], atoms), tall)
    summed = ((summed[:, 256:] + summed[:, 128:256]) + summed[:, :128]).T
    for i in range(3):
        part = jnp.sum(summed[i * ghosts : (i + 1) * ghosts], axis=0, keepdims=True)
        force_ref[i : i + 1, :] = -(grads_ref[i : i + 1, :] + part)
    total = strains[0][...]
    for other in strains[1:]:
        total = total + other[...]
    virial_ref[...] = -total[0:3, 0:3] / total[3:4, 0:1]


def call(body, inputs, outputs, scratch, scalars=()):
    where = [
        pl.BlockSpec(memory_space=pltpu.SMEM if i in scalars else pltpu.VMEM) for i in range(len(inputs))
    ]

    def kernel(*refs):
        body(refs)

    return pl.pallas_call(
        kernel,
        out_shape=[jax.ShapeDtypeStruct(s, d) for s, d in outputs],
        in_specs=where,
        out_specs=[pl.BlockSpec(memory_space=pltpu.VMEM)] * len(outputs),
        scratch_shapes=[pltpu.VMEM(s, d) for s, d in scratch],
        compiler_params=pltpu.CompilerParams(vmem_limit_bytes=40 * 2**20),
    )(*inputs)


class Plan:
    def __init__(self, sizes, ghosts, union):
        self.nx, self.ny, self.nz = sizes
        self.ghosts, self.union = ghosts, union
        groups = {}
        for q in range(9):
            oy, oz = q // 3 - 1, q % 3 - 1
            if q != 4:
                groups.setdefault((oy % self.ny, oz % self.nz), []).append(q)
        self.groups = list(groups.items())
        self.place = {q: (g, i) for g, (s, qs) in enumerate(self.groups) for i, q in enumerate(qs)}
        self.source = {q: g for q, (g, i) in self.place.items()}
        self.n_strain = 0

    def shift(self, value, dx, dy, dz):
        sizes = (self.nx, self.ny, self.nz)
        pairs = []
        for i in range(self.nx * self.ny * self.nz):
            x, y, z = np.unravel_index(i, sizes)
            to = ((x + dx) % sizes[0], (y + dy) % sizes[1], (z + dz) % sizes[2])
            pairs.append((i, int(np.ravel_multi_index(to, sizes))))
        if all(a == b for a, b in pairs):
            return value
        return lax.ppermute(value, AXES, pairs)

    def exchange(self, minus, zero, plus, sign, select, size):
        got_minus = self.shift(minus, -sign, 0, 0)
        got_plus = self.shift(plus, sign, 0, 0)
        out = [got_minus, got_plus]
        parts = (got_minus, zero, got_plus)
        whole = None if select else jnp.concatenate(parts, axis=0)
        for (sy, sz), qs in self.groups:
            payload = whole
            if select:
                payload = jnp.concatenate([p[q * size : (q + 1) * size] for q in qs for p in parts], axis=0)
            out.append(self.shift(payload, 0, sign * sy, sign * sz))
        return out


def shards(
    plan_sizes,
    positions,
    species,
    atom_count,
    export_union,
    ghost_map,
    edge_receiver,
    edge_sender,
    embed,
    species_energy,
    radial_in,
    radial_out,
    mixing,
    product,
    residual,
    read_one,
    read_hidden,
    read_two,
):
    atoms = positions.shape[-1]
    ghosts = ghost_map.shape[-1]
    union = export_union.shape[-1]
    edges = edge_receiver.shape[-1]
    channels = embed.shape[1]
    plan = Plan(plan_sizes, ghosts, union)
    lanes = 27 * ghosts
    slots = atoms + lanes
    third = 9 * ghosts
    count = atom_count.reshape(1)
    recv = edge_receiver.reshape(1, edges)
    send = edge_sender.reshape(1, edges)
    fill = jnp.zeros((4 * 128 - lanes - union,), F32)
    tail_rows = jnp.concatenate([ghost_map.reshape(-1).astype(F32), fill, export_union.reshape(-1).astype(F32)])
    own = jnp.concatenate(
        [positions.reshape(3, atoms), species.reshape(1, atoms).astype(F32), tail_rows.reshape(4, 128)], axis=0
    )

    swap = functools.partial(jnp.swapaxes, axis1=-1, axis2=-2)
    emb = wide_exact(jnp.pad(embed.T, ((0, 0), (0, 8 - embed.shape[0]))))
    energies = jnp.pad(species_energy, (0, 8 - embed.shape[0])).reshape(8, 1)
    rin = wide(swap(radial_in))
    rout = wide(swap(radial_out))
    mix = wide(swap(mixing))
    back_mix = wide(mixing)
    tail = jnp.concatenate([product, residual], axis=1)
    back_tail = wide(tail)
    tail = wide(swap(tail))
    read = wide(read_hidden.T)
    back_read = wide(read_hidden)
    one = read_one.reshape(channels, 1)
    two = read_two.reshape(-1, 1)

    before, after = plan.shift(own, 1, 0, 0), plan.shift(own, -1, 0, 0)
    column = jnp.concatenate([before, own, after], axis=0)
    packs = [before, own, after]
    for (sy, sz), qs in plan.groups:
        packs.append(plan.shift(column, 0, -sy, -sz))

    big = [((3 * channels, edges), F32)] * 2
    minus, zero, plus, h1, mixed, sep, energy, lists = call(
        functools.partial(first_kernel, plan),
        packs + [count, recv, send, emb, energies, rin[0], rout[0], mix[0], tail[0], one],
        [((third, channels), F32)] * 3
        + [
            ((channels, atoms), F32),
            ((9 * channels, atoms), F32),
            ((8, edges), F32),
            ((8, atoms), F32),
            ((8, lanes), jnp.int32),
        ],
        [
            ((216, 128), F32),
            ((8, edges), F32),
            ((8, edges), F32),
            ((1, edges), jnp.int32),
            *big,
            ((9 * channels, atoms), F32),
            ((1, edges), jnp.int32),
        ],
        scalars=(len(packs),),
    )
    got = plan.exchange(minus, zero, plus, -1, True, ghosts)
    minus, zero, plus, dlocal, base, edge, out_energy = call(
        functools.partial(second_kernel, plan),
        got
        + [count, recv, send, h1, sep, energy, rin[1], rout[1], mix[1], tail[1]]
        + [back_mix[1], back_tail[1], read, back_read, two, one],
        [((third, channels), F32)] * 3
        + [((atoms, channels), F32), ((channels, atoms), F32), ((8, edges), F32), ((8, atoms), F32)],
        [
            ((2 * channels, slots), BF16),
            ((8, edges), F32),
            ((8, edges), F32),
            ((1, edges), jnp.int32),
            *big,
            big[0],
            ((9 * channels, atoms), F32),
            ((9 * channels, atoms), F32),
            ((9 * channels, 2 * atoms), BF16),
            ((slots, 2 * channels), F32),
        ],
        scalars=(len(got),),
    )
    got = plan.exchange(minus, zero, plus, 1, True, ghosts)
    minus, zero, plus, grads, strain = call(
        functools.partial(third_kernel, plan),
        got
        + [count, recv, send, own, dlocal, base, edge, sep, mixed, lists, emb, rin[0], rout[0]]
        + [back_mix[0], back_tail[0]],
        [((16, 128), F32)] * 3 + [((8, atoms), F32), ((8, 128), F32)],
        [
            ((1, edges), jnp.int32),
            ((8, edges), F32),
            ((8, edges), F32),
            *big,
            ((9 * channels, 2 * atoms), BF16),
            ((8, edges), F32),
        ],
        scalars=(len(got),),
    )
    got = plan.exchange(minus, zero, plus, 1, False, 1)
    for axis, size in enumerate(plan_sizes):
        total = strain
        for d in range(1, size):
            step = [0, 0, 0]
            step[axis] = d
            total = total + plan.shift(strain, *step)
        strain = total
    plan.n_strain = 1
    forces, virial = call(
        functools.partial(last_kernel, plan),
        got + [strain, grads, lists],
        [((3, atoms), F32), ((3, 3), F32)],
        [],
    )
    return (forces[None, None, None], out_energy[0].reshape(1, 1, 1, atoms), virial)


def solution(mesh):
    sizes = tuple(mesh.shape[a] for a in AXES)
    return jax.shard_map(
        functools.partial(shards, sizes),
        mesh=mesh,
        in_specs=(
            P("gx", "gy", "gz", None, None),
            P("gx", "gy", "gz", None),
            P("gx", "gy", "gz"),
            P("gx", "gy", "gz", None),
            P("gx", "gy", "gz", None, None),
            P("gx", "gy", "gz", None),
            P("gx", "gy", "gz", None),
            *([P()] * 10),
        ),
        out_specs=(P("gx", "gy", "gz", None, None), P("gx", "gy", "gz", None), P()),
        check_vma=False,
    )
```

```python
import functools

import jax
import jax.numpy as jnp
import numpy as np
from jax import lax
from jax.experimental import pallas as pl
from jax.experimental.pallas import tpu as pltpu
from jax.sharding import PartitionSpec as P

DEG = 8
DOMAIN_SIDE = 5.0
SOFTENING = 0.25
RADIAL_RANGE = 18.0
R3 = 3.0**0.5
R5 = 5.0**0.5
R15 = 15.0**0.5
F32 = jnp.float32
BF16 = jnp.bfloat16
DEGREE = (0, 1, 1, 1, 2, 2, 2, 2, 2)
TILE = 256
VMEM_LIMIT = 20 * 2**20
AXES = ("gx", "gy", "gz")


def split(x, parts):
    out = []
    for i in range(parts):
        piece = x.astype(BF16)
        out.append(piece)
        if i + 1 < parts:
            x = x - piece.astype(F32)
    return out


def mm(a, b):
    return lax.dot_general(a, b, (((1,), (0,)), ((), ())), preferred_element_type=F32)


def mm_nt(a, b):
    return lax.dot_general(a, b, (((1,), (1,)), ((), ())), preferred_element_type=F32)


def stack3(x):
    hi, lo = split(x, 2)
    return jnp.concatenate([hi, hi, lo], axis=0)


def stack4(x):
    hi, lo = split(x, 2)
    return jnp.concatenate([hi, hi, lo, lo], axis=0)


def iota(shape, dim):
    return lax.broadcasted_iota(jnp.int32, shape, dim)


def onehot(row, size):
    return jnp.where(iota((size, row.shape[1]), 0) == row, 1.0, 0.0).astype(BF16)


def wide(x):
    hi, lo = split(x, 2)
    return jnp.concatenate([hi, lo, hi], axis=1)


def sin_cos(theta):
    shift = theta - np.float32(np.pi / 2)
    square = shift * shift
    even, odd = [1.0], [1.0]
    for n in range(1, 9):
        even.append(-even[-1] / ((2 * n - 1) * (2 * n)))
        odd.append(-odd[-1] / ((2 * n) * (2 * n + 1)))
    cos_shift = jnp.full_like(theta, even[-1])
    sin_shift = jnp.full_like(theta, odd[-1])
    for n in range(7, -1, -1):
        cos_shift = cos_shift * square + np.float32(even[n])
        sin_shift = sin_shift * square + np.float32(odd[n])
    return cos_shift, -(sin_shift * shift)


def geometry(sep):
    length = jnp.sqrt(sep[0] * sep[0] + sep[1] * sep[1] + sep[2] * sep[2] + SOFTENING)
    inverse = 1.0 / length
    return length, inverse, [s * inverse for s in sep]


def harmonics(unit):
    a, b, c = unit
    return [
        None,
        R3 * a,
        R3 * b,
        R3 * c,
        R15 * a * b,
        R15 * b * c,
        (0.5 * R5) * (3.0 * c * c - 1.0),
        R15 * a * c,
        (0.5 * R15) * (a * a - b * b),
    ]


def bases(length, inverse, count):
    step = np.float32(np.pi / RADIAL_RANGE)
    sine, cosine = sin_cos(length * step)
    twice = 2.0 * cosine
    s_before, s_now = jnp.zeros_like(sine), sine
    c_before, c_now = jnp.ones_like(sine), cosine
    front = np.float32((2.0 / RADIAL_RANGE) ** 0.5) * inverse
    values, slopes = [], []
    for n in range(1, count + 1):
        value = front * s_now
        values.append(value)
        slopes.append(front * (n * step) * c_now - value * inverse)
        s_before, s_now = s_now, twice * s_now - s_before
        c_before, c_now = c_now, twice * c_now - c_before
    return jnp.concatenate(values, axis=0), jnp.concatenate(slopes, axis=0)


def stack3_rows(x):
    hi = x.astype(BF16).astype(F32)
    return jnp.concatenate([hi, hi, x - hi], axis=0).astype(BF16)


def radial_net(rin, rout, value, slope):
    both = jnp.concatenate([stack3_rows(value), stack3_rows(slope)], axis=1)
    width = value.shape[1]
    first = mm(rin, both)
    pre, pre_slope = first[:, :width], first[:, width:]
    gate = 1.0 / (1.0 + jnp.exp(-pre))
    hidden = pre * gate
    hidden_slope = gate * (1.0 + pre * (1.0 - gate)) * pre_slope
    second = mm(rout, jnp.concatenate([stack4(hidden), stack4(hidden_slope)], axis=1))
    return second[:, :width], second[:, width:]


def rows_of(ref, where, count):
    block = ref[:, where]
    return [block[i : i + 1] for i in range(count)]


def forward_tile(where, sep_ref, live_row, weighted, agg_ref):
    channels = weighted[0].shape[0]
    length, inverse, unit = geometry(rows_of(sep_ref, where, 3))
    angular = harmonics(unit)
    pick = onehot(live_row, agg_ref.shape[1])
    pick = jnp.concatenate([pick, pick], axis=1)
    for m, l in enumerate(DEGREE):
        message = weighted[l] if m == 0 else weighted[l] * angular[m]
        part = slice(m * channels, (m + 1) * channels)
        agg_ref[part, :] += mm_nt(jnp.concatenate(split(message, 2), axis=1), pick)


def mix_forward(agg_ref, mixed_ref, mix_ref, tail_ref, h_local):
    channels, atoms = h_local.shape
    scale = float(DEG) ** -0.5
    squares = []
    for l, ms in enumerate(((0,), (1, 2, 3), (4, 5, 6, 7, 8))):
        stacked = jnp.concatenate([agg_ref[m * channels : (m + 1) * channels, :] * scale for m in ms], axis=1)
        mixed = mm(mix_ref[l], stack3(stacked))
        total = None
        for i, m in enumerate(ms):
            piece = mixed[:, i * atoms : (i + 1) * atoms]
            mixed_ref[m * channels : (m + 1) * channels, :] = piece
            term = piece if l == 0 else piece * piece
            total = term if total is None else total + term
        squares.append(total)
    return mm(tail_ref[...], stack3(jnp.concatenate(squares + [h_local], axis=0)))


def mix_backward(grad, mixed_ref, back_mix_ref, back_tail_ref, dagg_ref):
    channels, atoms = grad.shape
    scale = float(DEG) ** -0.5
    spread = mm(back_tail_ref[...], stack3(grad))
    for l, ms in enumerate(((0,), (1, 2, 3), (4, 5, 6, 7, 8))):
        base = spread[l * channels : (l + 1) * channels]
        pieces = []
        for m in ms:
            if l == 0:
                pieces.append(base * scale)
            else:
                pieces.append(base * (mixed_ref[m * channels : (m + 1) * channels, :] * (2.0 * scale)))
        out = mm(back_mix_ref[l], stack3(jnp.concatenate(pieces, axis=1)))
        for i, m in enumerate(ms):
            piece = out[:, i * atoms : (i + 1) * atoms]
            dagg_ref[m * channels : (m + 1) * channels, :] = jnp.concatenate(split(piece, 2), axis=1)
    return spread[3 * channels :]


def features_backward(where, sep_ref, live_row, dagg_ref, rad_ref):
    channels, atoms = dagg_ref.shape[0] // 9, dagg_ref.shape[1] // 2
    length, inverse, unit = geometry(rows_of(sep_ref, where, 3))
    angular = harmonics(unit)
    pick = onehot(live_row, atoms)
    pick = jnp.concatenate([pick, pick], axis=0)
    by_weight = [None, None, None]
    for m, l in enumerate(DEGREE):
        grad = mm(dagg_ref[m * channels : (m + 1) * channels, :], pick)
        term = grad if m == 0 else grad * angular[m]
        by_weight[l] = term if by_weight[l] is None else by_weight[l] + term
    parts = [by_weight[l] * rad_ref[l * channels : (l + 1) * channels, where] for l in range(3)]
    return parts[0] + parts[1] + parts[2]


def geometry_backward(where, sep_ref, live_row, dagg_ref, weighted, slopes, out_ref):
    channels, atoms = dagg_ref.shape[0] // 9, dagg_ref.shape[1] // 2
    length, inverse, unit = geometry(rows_of(sep_ref, where, 3))
    angular = harmonics(unit)
    pick = onehot(live_row, atoms)
    pick = jnp.concatenate([pick, pick], axis=0)
    by_weight = [None, None, None]
    p = [None] * 9
    for m, l in enumerate(DEGREE):
        grad = mm(dagg_ref[m * channels : (m + 1) * channels, :], pick)
        term = grad if m == 0 else grad * angular[m]
        by_weight[l] = term if by_weight[l] is None else by_weight[l] + term
        if m:
            p[m] = jnp.sum(grad * weighted[l], axis=0, keepdims=True)
    total = by_weight[0] * slopes[0] + by_weight[1] * slopes[1] + by_weight[2] * slopes[2]
    by_length = jnp.sum(total, axis=0, keepdims=True)
    a, b, c = unit
    by_unit = [
        R3 * p[1] + R15 * (b * p[4] + c * p[7] + a * p[8]),
        R3 * p[2] + R15 * (a * p[4] + c * p[5] - b * p[8]),
        R3 * p[3] + R15 * (b * p[5] + a * p[7]) + (3.0 * R5) * c * p[6],
    ]
    along = a * by_unit[0] + b * by_unit[1] + c * by_unit[2]
    for i in range(3):
        out_ref[i : i + 1, where] = (by_unit[i] - unit[i] * along) * inverse + by_length * unit[i]


def live_receiver(recv, count):
    return jnp.where(iota(recv.shape, 1) < DEG * count, recv, -1)


def tiles(total, body):
    def step(i, carry):
        body(pl.ds(pl.multiple_of(i * TILE, TILE), TILE))
        return carry

    lax.fori_loop(0, total // TILE, step, 0)


def pack_kernel(refs):
    position_ref, species_ref, union_ref, lists_ref, out_ref = refs
    ghosts, blocks = lists_ref.shape
    union = union_ref.shape[1]
    spread = jnp.where(iota((blocks, 512), 0) == iota((blocks, 512), 1) // ghosts, 1.0, 0.0).astype(BF16)
    tall = mm(lists_ref[...].astype(F32).astype(BF16), spread)
    tall = jnp.where(iota((ghosts, 512), 0) == iota((ghosts, 512), 1) % ghosts, tall, 0.0)
    place = jnp.where(iota((union, 512), 0) + (512 - union) == iota((union, 512), 1), 1.0, 0.0).astype(BF16)
    offered = mm(jnp.broadcast_to(union_ref[...].astype(F32), (8, union)).astype(BF16), place)
    flat = jnp.sum(tall, axis=0, keepdims=True) + offered[0:1]
    for i in range(3):
        out_ref[i : i + 1, :] = position_ref[i]
    out_ref[3:4, :] = species_ref[...].astype(F32)
    for r in range(4):
        out_ref[4 + r : 5 + r, :] = flat[:, 128 * r : 128 * r + 128]


def prep_kernel(refs):
    (embed_ref, energy_ref, rin_ref, rout_ref, mix_ref, product_ref, residual_ref, one_ref, read_ref, two_ref) = refs[:10]
    recv_ref, send_ref, count_ref = refs[10:13]
    (emb_out, energy_out, one_out, two_out, read_out, back_read_out, live_out, send_out) = refs[13:21]
    layers = refs[21:-1]
    live_out[...] = live_receiver(recv_ref[...], count_ref[0])
    send_out[...] = send_ref[...]
    square = refs[-1]
    channels = residual_ref.shape[1]

    def turn(pieces, rows):
        square[...] = jnp.zeros_like(square)
        for at, piece in pieces:
            square[at : at + piece.shape[0], 0 : piece.shape[1]] = piece
        return square[...].T[:rows]

    def halves(x):
        hi = x.astype(BF16).astype(F32)
        return hi, x - hi

    hi, rest = halves(embed_ref[...])
    mid, low = halves(rest)
    emb_out[...] = turn([(0, hi), (8, mid), (16, low)], channels)[:, :24].astype(BF16)
    count = energy_ref.shape[1]
    energy_out[...] = jnp.sum(
        jnp.where(iota((8, count), 0) == iota((8, count), 1), energy_ref[...], 0.0), axis=1, keepdims=True
    )
    width = two_ref.shape[1]
    two_out[...] = jnp.sum(
        jnp.where(iota((width, width), 0) == iota((width, width), 1), two_ref[...], 0.0), axis=1, keepdims=True
    )
    one_out[...] = jnp.sum(
        jnp.where(iota((channels, channels), 0) == iota((channels, channels), 1), one_ref[...], 0.0),
        axis=1,
        keepdims=True,
    )
    read_out[...] = wide(read_ref[...])
    hi, low = halves(read_ref[...])
    back_read_out[...] = turn([(0, hi), (width, low), (2 * width, hi)], channels)[:, : 3 * width].astype(BF16)
    for t in range(2):
        rin_out, rout_out, mix_out, back_mix_out, tail_out, back_tail_out = layers[6 * t : 6 * t + 6]
        hi, low = halves(rin_ref[t])
        n = hi.shape[0]
        rin_out[...] = turn([(0, hi), (n, low), (2 * n, hi)], hi.shape[1])[:, : 3 * n].astype(BF16)
        hi, low = halves(rout_ref[t])
        rout_out[...] = jnp.concatenate([hi, low, hi, low], axis=0).T.astype(BF16)
        for l in range(3):
            back_mix_out[l] = wide(mix_ref[t, l])
            mix_out[l] = wide(mix_ref[t, l].T)
        tail = jnp.concatenate([product_ref[t], residual_ref[t]], axis=0)
        back_tail_out[...] = wide(tail)
        tail_out[...] = wide(tail.T)


def first_kernel(plan, refs):
    n_in = len(plan.groups) + 3
    packs, refs = refs[:n_in], refs[n_in:]
    (live_ref, send_ref, emb_ref, se_ref, rin_ref, rout_ref, mix_ref, tail_ref, one_ref) = refs[:9]
    (minus_ref, zero_ref, plus_ref, h_ref, mixed_ref, sep_ref, energy_ref, list_ref, w_ref, wp_ref) = refs[9:19]
    all_ref, basis_ref, slope_ref, agg_ref, species_ref = refs[19:]
    ghosts, union = plan.ghosts, plan.union
    blocks = 27
    lanes = blocks * ghosts
    atoms = agg_ref.shape[1]
    own = packs[1][...]
    for k in range(blocks):
        i, q = k // 9, k % 9
        if q == 4:
            piece = packs[i][...]
        else:
            piece = packs[3 + plan.source[q]][8 * i : 8 * i + 8, :]
        all_ref[8 * k : 8 * k + 8, :] = piece
    flat = (iota((8, 128), 0) - 4) * 128 + iota((8, 128), 1)
    asked = jnp.zeros((8, 128), F32)
    for k in range(blocks):
        lo = (26 - k) * ghosts
        asked = jnp.where((flat >= lo) & (flat < lo + ghosts), all_ref[8 * k : 8 * k + 8, :], asked)

    def flat_lists(pack):
        rows = jnp.concatenate([pack[r : r + 1] for r in range(4, 8)], axis=1)
        return rows[:, :lanes].astype(jnp.int32)

    offers = mm(all_ref[...].astype(BF16), onehot(flat_lists(own) + (128 - union), 128))
    block_of = iota((8, lanes), 1) // ghosts
    chosen = jnp.zeros((8, lanes), F32)
    for k in range(blocks):
        chosen = jnp.where(block_of == k, offers[8 * k : 8 * k + 8], chosen)
    ghost_atom = chosen[7:8].astype(jnp.int32)
    mine = mm(own.astype(BF16), onehot(flat_lists(asked) + (128 - union), 128))
    send_atom = mine[7:8].astype(jnp.int32)
    list_ref[...] = jnp.broadcast_to(send_atom, (8, lanes))
    found = None
    pick = onehot(ghost_atom, 128)
    for piece in split(all_ref[...], 3):
        term = mm(piece, pick)
        found = term if found is None else found + term
    table = jnp.zeros((8, lanes), F32)
    row = iota((8, lanes), 0)
    for k in range(blocks):
        table = jnp.where(block_of == k, found[8 * k : 8 * k + 8], table)
    offset = jnp.where(row == 0, block_of // 9 - 1, jnp.where(row == 1, block_of // 3 % 3 - 1, block_of % 3 - 1))
    table = jnp.where(row < 3, table + DOMAIN_SIDE * offset.astype(F32), table)
    table = jnp.concatenate([own, table], axis=1)
    table = jnp.concatenate(split(table, 3), axis=0)
    own3 = jnp.concatenate(split(own, 3), axis=0)
    edges = live_ref.shape[1]
    from_sender = mm(table, onehot(send_ref[...], table.shape[1]))
    at_receiver = mm(own3, onehot(live_ref[...], atoms))
    from_sender = (from_sender[16:] + from_sender[8:16]) + from_sender[:8]
    at_receiver = (at_receiver[16:] + at_receiver[8:16]) + at_receiver[:8]
    sep_ref[...] = from_sender - jnp.where(iota((8, edges), 0) < 3, at_receiver, 0.0)
    species_ref[...] = from_sender[3:4].astype(jnp.int32)
    length, inverse, unit = geometry([sep_ref[i : i + 1, :] for i in range(3)])
    value, slope = bases(length, inverse, rin_ref.shape[1] // 3)
    basis_ref[...] = value
    slope_ref[...] = slope
    agg_ref[...] = jnp.zeros_like(agg_ref)

    def species_features(row):
        hot = jnp.where(iota((8, row.shape[1]), 0) == row, 1.0, 0.0)
        return mm(emb_ref[...], jnp.concatenate([hot, hot, hot], axis=0).astype(BF16)), hot

    def body(where):
        features, unused = species_features(species_ref[:, where])
        rad, rad_slope = radial_net(rin_ref[...], rout_ref[...], basis_ref[:, where], slope_ref[:, where])
        channels = features.shape[0]
        weighted = []
        for l in range(3):
            part = slice(l * channels, (l + 1) * channels)
            weighted.append(rad[part] * features)
            w_ref[part, where] = weighted[l]
            wp_ref[part, where] = rad_slope[part] * features
        forward_tile(where, sep_ref, live_ref[:, where], weighted, agg_ref)

    tiles(edges, body)
    h0, hot = species_features(own[3:4].astype(jnp.int32))
    h1 = mix_forward(agg_ref, mixed_ref, mix_ref, tail_ref, h0)
    h_ref[...] = h1
    parts = split(h1, 2)
    chosen_h = mm_nt(onehot_rows(send_atom, atoms), jnp.concatenate(parts, axis=0))
    chosen_h = chosen_h[:, :128] + chosen_h[:, 128:]
    third = 9 * ghosts
    minus_ref[...] = chosen_h[:third]
    zero_ref[...] = chosen_h[third : 2 * third]
    plus_ref[...] = chosen_h[2 * third :]
    energy = jnp.sum(hot * se_ref[...], axis=0, keepdims=True) + jnp.sum(h1 * one_ref[...], axis=0, keepdims=True)
    energy_ref[...] = jnp.broadcast_to(energy, (8, atoms))


def onehot_rows(row, size):
    hot = jnp.where(iota((size, row.shape[1]), 0) == row, 1.0, 0.0)
    pad = (-row.shape[1]) % 128
    if pad:
        hot = jnp.concatenate([hot, jnp.zeros((size, pad), F32)], axis=1)
    return hot.T[: row.shape[1]].astype(BF16)


def radial_kernel(refs):
    sep_ref, rin_ref, rout_ref, rad_ref, rad_slope_ref, basis_ref, slope_ref = refs
    length, inverse, unit = geometry([sep_ref[i : i + 1, :] for i in range(3)])
    value, slope = bases(length, inverse, rin_ref.shape[1] // 3)
    basis_ref[...] = value
    slope_ref[...] = slope

    def body(where):
        rad, rad_slope = radial_net(rin_ref[...], rout_ref[...], basis_ref[:, where], slope_ref[:, where])
        rad_ref[:, where] = rad
        rad_slope_ref[:, where] = rad_slope

    tiles(sep_ref.shape[1], body)


def second_kernel(plan, refs):
    n_in = len(plan.groups) + 2
    got, refs = refs[:n_in], refs[n_in:]
    (count_ref, live_ref, send_ref, h_ref, sep_ref, energy_ref, rad_ref, mix_ref, tail_ref) = refs[:9]
    (back_mix_ref, back_tail_ref, read_ref, back_read_ref, two_ref, one_ref) = refs[9:15]
    (minus_ref, zero_ref, plus_ref, dlocal_ref, base_ref, out_energy_ref, feature_ref, dagg_ref) = refs[15:23]
    table_ref, agg_ref, mixed_ref, dt_ref = refs[23:]
    ghosts = plan.ghosts
    atoms = agg_ref.shape[1]
    channels = h_ref.shape[0]
    count = count_ref[0]
    edges = live_ref.shape[1]
    h1 = h_ref[...]
    table_ref[:, :atoms] = jnp.concatenate(split(h1, 2), axis=0)
    rows = ghost_rows(plan, got, ghosts, channels)
    lanes = 27 * ghosts
    pad = (-lanes) % 128
    ghost = jnp.concatenate(rows + [jnp.zeros((pad, channels), F32)], axis=0).T
    table_ref[:, atoms:] = jnp.concatenate(split(ghost, 2), axis=0)[:, :lanes]
    agg_ref[...] = jnp.zeros_like(agg_ref)
    slots = atoms + lanes

    def body(where):
        features = mm(table_ref[...], onehot(send_ref[:, where], slots))
        features = features[:channels] + features[channels:]
        feature_ref[:, where] = features
        weighted = [rad_ref[l * channels : (l + 1) * channels, where] * features for l in range(3)]
        forward_tile(where, sep_ref, live_ref[:, where], weighted, agg_ref)

    tiles(edges, body)
    h2 = mix_forward(agg_ref, mixed_ref, mix_ref, tail_ref, h1)
    pre = mm(read_ref[...], stack3(h2))
    gate = 1.0 / (1.0 + jnp.exp(-pre))
    live = jnp.where(iota((1, atoms), 1) < count, 1.0, 0.0)
    energy_two = jnp.sum(two_ref[...] * (pre * gate), axis=0, keepdims=True)
    out_energy_ref[...] = (energy_ref[0:1, :] + energy_two) * live
    grad_pre = two_ref[...] * (gate * (1.0 + pre * (1.0 - gate))) * live
    grad = mm(back_read_ref[...], stack3(grad_pre))
    base_ref[...] = mix_backward(grad, mixed_ref, back_mix_ref, back_tail_ref, dagg_ref) + one_ref[...] * live
    dt_ref[...] = jnp.zeros_like(dt_ref)

    def back(where):
        feature_grad = features_backward(where, sep_ref, live_ref[:, where], dagg_ref, rad_ref)
        dt_ref[...] += mm_nt(onehot(send_ref[:, where], slots), jnp.concatenate(split(feature_grad, 2), axis=0))

    tiles(edges, back)
    grads = dt_ref[:, :channels] + dt_ref[:, channels:]
    third = 9 * ghosts
    dlocal_ref[...] = grads[:atoms]
    minus_ref[...] = grads[atoms : atoms + third]
    zero_ref[...] = grads[atoms + third : atoms + 2 * third]
    plus_ref[...] = grads[atoms + 2 * third :]


def edge_kernel(refs):
    live_ref, sep_ref, rad_ref, rad_slope_ref, feature_ref, dagg_ref, edge_ref = refs
    channels = feature_ref.shape[0]
    edge_ref[...] = jnp.zeros_like(edge_ref)

    def body(where):
        features = feature_ref[:, where]
        parts = [slice(l * channels, (l + 1) * channels) for l in range(3)]
        weighted = [rad_ref[p, where] * features for p in parts]
        slopes = [rad_slope_ref[p, where] * features for p in parts]
        geometry_backward(where, sep_ref, live_ref[:, where], dagg_ref, weighted, slopes, edge_ref)

    tiles(live_ref.shape[1], body)


def ghost_rows(plan, got, size, width):
    rows = []
    for k in range(27):
        i, q = k // 9, k % 9
        if k == 13:
            rows.append(jnp.zeros((size, width), F32))
        elif q == 4:
            rows.append(got[0 if i == 0 else 1][4 * size : 5 * size, :])
        else:
            group, place = plan.place[q]
            at = (3 * place + i) * size
            rows.append(got[2 + group][at : at + size, :])
    return rows


def third_kernel(plan, refs):
    n_in = len(plan.groups) + 2
    got, refs = refs[:n_in], refs[n_in:]
    (count_ref, live_ref, send_ref, own_ref, dlocal_ref, base_ref, edge_in_ref, sep_ref, mixed_ref, list_ref) = refs[:10]
    (w_ref, wp_ref, back_mix_ref, back_tail_ref) = refs[10:14]
    minus_ref, zero_ref, plus_ref, grads_ref = refs[14:18]
    dagg_ref, edge_ref = refs[18:]
    ghosts = plan.ghosts
    atoms = own_ref.shape[1]
    channels = base_ref.shape[0]
    edges = live_ref.shape[1]
    lanes = 27 * ghosts
    count = count_ref[0]
    returned = jnp.concatenate(ghost_rows(plan, got, ghosts, channels), axis=0)
    pick = onehot(list_ref[0:1, :], atoms)
    back = mm(pick, jnp.concatenate(split(returned, 2), axis=1))
    back = dlocal_ref[...] + back[:, :channels] + back[:, channels:]
    grad = base_ref[...] + back.T
    mix_backward(grad, mixed_ref, back_mix_ref, back_tail_ref, dagg_ref)

    def body(where):
        parts = [slice(l * channels, (l + 1) * channels) for l in range(3)]
        weighted = [w_ref[p, where] for p in parts]
        slopes = [wp_ref[p, where] for p in parts]
        geometry_backward(where, sep_ref, live_ref[:, where], dagg_ref, weighted, slopes, edge_ref)

    tiles(edges, body)
    edge = [edge_ref[i : i + 1, :] + edge_in_ref[i : i + 1, :] for i in range(3)]
    sep = [sep_ref[i : i + 1, :] for i in range(3)]
    sender = send_ref[...]
    by_atom = jnp.where(iota((atoms, edges), 0) == sender, 1.0, 0.0) - jnp.where(
        iota((atoms, edges), 0) == live_ref[...], 1.0, 0.0
    )
    five = [jnp.zeros_like(edge[0])] * 5
    stacked = jnp.concatenate(split(jnp.concatenate(edge + five, axis=0), 3), axis=0)
    sums = mm_nt(stacked, by_atom.astype(BF16))
    grads_ref[...] = (sums[16:] + sums[8:16]) + sums[:8]
    ghost = sender - atoms
    block = jnp.where(ghost >= 0, ghost // ghosts, -1)
    slot = ghost % ghosts
    slot_hot = jnp.where(iota((ghosts, edges), 0) == slot, 1.0, 0.0)
    spread = jnp.concatenate([g * slot_hot for g in edge], axis=0)
    pad = jnp.zeros((128 - 3 * ghosts, edges), F32)
    pieces = split(jnp.concatenate([spread, pad], axis=0), 3)
    for i, out in enumerate((minus_ref, zero_ref, plus_ref)):
        rows = iota((16, edges), 0)
        hot = jnp.where((rows + 9 * i == block) & (rows < 9), 1.0, 0.0).astype(BF16)
        sums = [mm_nt(hot, piece) for piece in pieces]
        out[...] = (sums[2] + sums[1]) + sums[0]
    lane = iota((1, 128), 1)
    packed = jnp.where(lane == 9, count.astype(F32), 0.0)
    for i in range(3):
        for j in range(3):
            packed = jnp.where(lane == 3 * i + j, jnp.sum(edge[i] * sep[j]), packed)
    for out in (minus_ref, zero_ref, plus_ref):
        out[9:10, :] = packed


def last_kernel(plan, refs):
    n_in = len(plan.groups) + 2
    got, refs = refs[:n_in], refs[n_in:]
    strain_ref, grads_ref, list_ref, force_ref, virial_ref = refs
    ghosts = plan.ghosts
    lanes = 27 * ghosts
    atoms = grads_ref.shape[1]
    rows = []
    for k in range(27):
        i, q = k // 9, k % 9
        if k == 13:
            rows.append(jnp.zeros((1, 128), F32))
        elif q == 4:
            rows.append(got[0 if i == 0 else 1][4:5, :])
        else:
            at = 16 * i + q
            rows.append(got[2 + plan.place[q][0]][at : at + 1, :])
    block = jnp.concatenate(rows + [jnp.zeros((5, 128), F32)], axis=0)
    block = jnp.concatenate(split(block, 3), axis=1)
    repeat = jnp.where(iota((lanes, 32), 0) // ghosts == iota((lanes, 32), 1), 1.0, 0.0).astype(BF16)
    tall = mm(repeat, block)
    keep = iota((lanes, 384), 0) % ghosts == iota((lanes, 384), 1) % ghosts
    tall = jnp.where(keep, tall, 0.0).astype(BF16)
    summed = mm(onehot(list_ref[0:1, :], atoms), tall)
    summed = ((summed[:, 256:] + summed[:, 128:256]) + summed[:, :128]).T
    for i in range(3):
        part = jnp.sum(summed[i * ghosts : (i + 1) * ghosts], axis=0, keepdims=True)
        force_ref[i] = -(grads_ref[i : i + 1, :] + part)
    total = strain_ref[0:1, :]
    if plan.plane_direct:
        for ref in got[2:]:
            total = total + ref[48:49, :]
    ratio = -total / total[:, 9:10]
    for i in range(3):
        virial_ref[i : i + 1, :] = ratio[:, 3 * i : 3 * i + 3]


def call(body, inputs, outputs, scratch, scalars=(), loads=0, work=0):
    where = [pl.BlockSpec(memory_space=pltpu.VMEM)] * len(inputs)
    for i in scalars:
        where[i] = pl.BlockSpec(memory_space=pltpu.SMEM)
    for i in range(loads):
        where[i] = pl.BlockSpec(memory_space=pltpu.HBM)
    shapes = [pltpu.VMEM(s, d) for s, d in scratch]
    inputs = [pltpu.with_memory_space_constraint(x, pltpu.HBM) if i < loads else x for i, x in enumerate(inputs)]
    if loads:
        shapes += [pltpu.VMEM(x.shape, x.dtype) for x in inputs[:loads]] + [pltpu.SemaphoreType.DMA((loads,))]

    def kernel(*refs):
        if loads:
            refs, held, sems = refs[: -loads - 1], refs[-loads - 1 : -1], refs[-1]
            copies = [pltpu.make_async_copy(refs[i], held[i], sems.at[i]) for i in range(loads)]
            for copy in copies:
                copy.start()
            for copy in copies:
                copy.wait()
            refs = tuple(held) + tuple(refs[loads:])
        body(refs)

    return pl.pallas_call(
        kernel,
        out_shape=[jax.ShapeDtypeStruct(s, d) for s, d in outputs],
        in_specs=where,
        out_specs=[pl.BlockSpec(memory_space=pltpu.VMEM)] * len(outputs),
        scratch_shapes=shapes,
        cost_estimate=pl.CostEstimate(flops=work * 10**9, bytes_accessed=10**5, transcendentals=0) if work else None,
        compiler_params=pltpu.CompilerParams(vmem_limit_bytes=VMEM_LIMIT),
    )(*inputs)


class Plan:
    def __init__(self, sizes, ghosts, union):
        self.nx, self.ny, self.nz = sizes
        self.ghosts, self.union = ghosts, union
        groups = {}
        for q in range(9):
            oy, oz = q // 3 - 1, q % 3 - 1
            if q != 4:
                groups.setdefault((oy % self.ny, oz % self.nz), []).append(q)
        self.groups = list(groups.items())
        self.place = {q: (g, i) for g, (s, qs) in enumerate(self.groups) for i, q in enumerate(qs)}
        self.source = {q: g for q, (g, i) in self.place.items()}
        self.plane_direct = self.ny * self.nz - 1 - len(self.groups) <= 4

    def shift(self, value, dx, dy, dz):
        sizes = (self.nx, self.ny, self.nz)
        pairs = []
        for i in range(self.nx * self.ny * self.nz):
            x, y, z = np.unravel_index(i, sizes)
            to = ((x + dx) % sizes[0], (y + dy) % sizes[1], (z + dz) % sizes[2])
            pairs.append((i, int(np.ravel_multi_index(to, sizes))))
        if all(a == b for a, b in pairs):
            return value
        return lax.ppermute(value, AXES, pairs)

    def last_exchange(self, minus, zero, plus):
        got_minus = self.shift(minus, -1, 0, 0)
        got_plus = self.shift(plus, 1, 0, 0)
        total = zero[8:16]
        if self.nx > 1:
            total = total + got_minus[8:16]
        if self.nx > 2:
            total = total + got_plus[8:16]
        for d in range(2, self.nx - 1):
            total = total + self.shift(zero[8:16], d, 0, 0)
        total = jnp.concatenate([total[1:], total[:1]], axis=0)
        payload = jnp.concatenate([got_minus, zero, got_plus, total], axis=0)
        out = [got_minus, got_plus]
        for (sy, sz), qs in self.groups:
            out.append(self.shift(payload, 0, sy, sz))
        if self.plane_direct:
            near = [s for s, qs in self.groups]
            own = total
            for sy in range(self.ny):
                for sz in range(self.nz):
                    if (sy, sz) != (0, 0) and (sy, sz) not in near:
                        total = total + self.shift(own, 0, sy, sz)
        else:
            for axis, size in ((1, self.ny), (2, self.nz)):
                own = total
                for d in range(1, size):
                    total = total + self.shift(own, 0, d * (axis == 1), d * (axis == 2))
        return out, total

    def exchange(self, minus, zero, plus, sign, size, side):
        got_minus = self.shift(minus, -sign, 0, 0)
        got_plus = self.shift(plus, sign, 0, 0)
        got_minus, got_plus, *side = lax.optimization_barrier((got_minus, got_plus, *side))
        out = [got_minus, got_plus]
        parts = (got_minus, zero, got_plus)
        for (sy, sz), qs in self.groups:
            payload = jnp.concatenate([p[q * size : (q + 1) * size] for q in qs for p in parts], axis=0)
            out.append(self.shift(payload, 0, sign * sy, sign * sz))
        return out, side


def shards(
    plan_sizes,
    positions,
    species,
    atom_count,
    export_union,
    ghost_map,
    edge_receiver,
    edge_sender,
    embed,
    species_energy,
    radial_in,
    radial_out,
    mixing,
    product,
    residual,
    read_one,
    read_hidden,
    read_two,
):
    atoms = positions.shape[-1]
    ghosts = ghost_map.shape[-1]
    union = export_union.shape[-1]
    edges = edge_receiver.shape[-1]
    channels = embed.shape[1]
    plan = Plan(plan_sizes, ghosts, union)
    lanes = 27 * ghosts
    slots = atoms + lanes
    third = 9 * ghosts
    count = atom_count.reshape(1)
    recv = edge_receiver.reshape(1, edges)
    send = edge_sender.reshape(1, edges)
    asked = jnp.swapaxes(ghost_map.reshape(27, ghosts), 0, 1)
    (own,) = call(
        pack_kernel,
        [positions.reshape(3, 1, atoms), species.reshape(1, atoms), export_union.reshape(1, union), asked],
        [((8, 128), F32)],
        [],
        loads=4,
    )
    species_count, n_basis, hidden = embed.shape[0], radial_in.shape[1], radial_in.shape[2]
    read_width = read_hidden.shape[1]
    layer = [
        ((hidden, 3 * n_basis), BF16),
        ((3 * channels, 4 * hidden), BF16),
        ((3, channels, 3 * channels), BF16),
        ((3, channels, 3 * channels), BF16),
        ((channels, 12 * channels), BF16),
        ((4 * channels, 3 * channels), BF16),
    ]
    emb, energies, one, two, read, back_read, live, send, *layers = call(
        prep_kernel,
        [embed, species_energy.reshape(1, species_count), radial_in, radial_out, mixing, product, residual]
        + [read_one.reshape(1, channels), read_hidden.T, read_two.reshape(1, read_width), recv, send, count],
        [
            ((channels, 24), BF16),
            ((8, 1), F32),
            ((channels, 1), F32),
            ((read_width, 1), F32),
            ((read_width, 3 * channels), BF16),
            ((channels, 3 * read_width), BF16),
            ((1, edges), jnp.int32),
            ((1, edges), jnp.int32),
            *layer,
            *layer,
        ],
        [((128, 128), F32)],
        scalars=(12,),
        loads=12,
        work=2,
    )

    before, after = plan.shift(own, 1, 0, 0), plan.shift(own, -1, 0, 0)
    before, after, emb, live, send, *layers = lax.optimization_barrier((before, after, emb, live, send, *layers))
    rin, rout, mix, back_mix, tail, back_tail = zip(layers[:6], layers[6:])
    column = jnp.concatenate([before, own, after], axis=0)
    packs = [before, own, after]
    for (sy, sz), qs in plan.groups:
        packs.append(plan.shift(column, 0, -sy, -sz))

    big = [((3 * channels, edges), F32)] * 2
    minus, zero, plus, h1, mixed, sep, energy, lists, w0, wp0 = call(
        functools.partial(first_kernel, plan),
        packs + [live, send, emb, energies, rin[0], rout[0], mix[0], tail[0], one],
        [((third, channels), F32)] * 3
        + [
            ((channels, atoms), F32),
            ((9 * channels, atoms), F32),
            ((8, edges), F32),
            ((8, atoms), F32),
            ((8, lanes), jnp.int32),
            *big,
        ],
        [
            ((216, 128), F32),
            ((8, edges), F32),
            ((8, edges), F32),
            ((9 * channels, atoms), F32),
            ((1, edges), jnp.int32),
        ],
    )
    side = call(radial_kernel, [sep, rin[1], rout[1]], big, [((8, edges), F32)] * 2, work=2)
    got, (rad, rad_slope) = plan.exchange(minus, zero, plus, -1, ghosts, side)
    minus, zero, plus, dlocal, base, out_energy, features, dagg = call(
        functools.partial(second_kernel, plan),
        got
        + [count, live, send, h1, sep, energy, rad, mix[1], tail[1]]
        + [back_mix[1], back_tail[1], read, back_read, two, one],
        [((third, channels), F32)] * 3
        + [((atoms, channels), F32), ((channels, atoms), F32), ((1, atoms), F32), ((channels, edges), F32)]
        + [((9 * channels, 2 * atoms), BF16)],
        [
            ((2 * channels, slots), BF16),
            ((9 * channels, atoms), F32),
            ((9 * channels, atoms), F32),
            ((slots, 2 * channels), F32),
        ],
        scalars=(len(got),),
    )
    side = call(edge_kernel, [live, sep, rad, rad_slope, features, dagg], [((8, edges), F32)], [], work=2)
    got, (edge,) = plan.exchange(minus, zero, plus, 1, ghosts, side)
    minus, zero, plus, grads = call(
        functools.partial(third_kernel, plan),
        got
        + [count, live, send, own, dlocal, base, edge, sep, mixed, lists, w0, wp0]
        + [back_mix[0], back_tail[0]],
        [((16, 128), F32)] * 3 + [((8, atoms), F32)],
        [((9 * channels, 2 * atoms), BF16), ((8, edges), F32)],
        scalars=(len(got),),
    )
    got, strain = plan.last_exchange(minus, zero, plus)
    forces, virial = call(
        functools.partial(last_kernel, plan), got + [strain, grads, lists], [((3, 1, atoms), F32), ((3, 3), F32)], []
    )
    return (forces.reshape(1, 1, 1, 3, atoms), out_energy.reshape(1, 1, 1, atoms), virial)


def solution(mesh):
    sizes = tuple(mesh.shape[a] for a in AXES)
    return jax.shard_map(
        functools.partial(shards, sizes),
        mesh=mesh,
        in_specs=(
            P("gx", "gy", "gz", None, None),
            P("gx", "gy", "gz", None),
            P("gx", "gy", "gz"),
            P("gx", "gy", "gz", None),
            P("gx", "gy", "gz", None, None),
            P("gx", "gy", "gz", None),
            P("gx", "gy", "gz", None),
            *([P()] * 10),
        ),
        out_specs=(P("gx", "gy", "gz", None, None), P("gx", "gy", "gz", None), P()),
        check_vma=False,
    )
```
